32 devices in a mesh: groups: 2 (over y), row: 4 (over z), col: 4 (over x, core).
Axes of the slice: x: 2, y: 2, z: 4, core: 2. Of those that a mesh axis runs over, the one named last changes fastest.
Arguments:
- tokens: bfloat16 [512, 8192], P(('groups', 'row'), 'col'), parts along dimension 0, may hold values from -6 to 6
- codes_gate: bfloat16 [8192, 28672], P('col', 'row'), may hold values from 0 to 3, as said below
- codes_up: bfloat16 [8192, 28672], P('col', 'row'), may hold values from 0 to 3, as said below
- scale_gate: float32 [64, 28672], P('col', 'row'), may hold values from 0.003 to 0.03
- offset_gate: float32 [64, 28672], P('col', 'row'), may hold values from 0 to 0.03
- scale_up: float32 [64, 28672], P('col', 'row'), may hold values from 0.003 to 0.03
- offset_up: float32 [64, 28672], P('col', 'row'), may hold values from 0 to 0.03
- grad_hidden: bfloat16 [512, 28672], P(('groups', 'col'), 'row'), parts along dimension 0, may hold values from -0.046875 to 0.046875
Outputs:
- hidden: bfloat16 [512, 28672], P(('groups', 'col'), 'row'), parts along dimension 0
- grad_scale_gate: float32 [128, 28672], P(('groups', 'col'), 'row'), parts along dimension 0
- grad_offset_gate: float32 [128, 28672], P(('groups', 'col'), 'row'), parts along dimension 0
- grad_scale_up: float32 [128, 28672], P(('groups', 'col'), 'row'), parts along dimension 0
- grad_offset_up: float32 [128, 28672], P(('groups', 'col'), 'row'), parts along dimension 0
The draws below stay inside these ranges and needn't reach their ends.
There are 2 independent parts, one for each index of `groups`. The reference program is written for one: setup_inputs(seed, part) draws one part's arguments, and reference() takes and returns one part's arrays. A program takes and returns all parts, laid end to end along the dimension named above; an argument that names none is the same for every part. Nothing has to cross between parts.
Inputs may be any that keep to these rules, and one draw needn't show every extreme that they name: `codes_gate`: whole numbers held as bfloat16. `codes_up`: whole numbers held as bfloat16.
All inputs are finite; a program needn't handle non-finite values.
Results may differ from the reference program's by a relative error of at most 0.006.
Values may be sent and summed in bfloat16 or wider, within the bound.
A program may use at most 256 MiB of HBM per device.

```python
import math
import jax
import jax.numpy as jnp
from jax import lax

D = 8192
FF = 28672
GROUP = 128
TOKENS = 256


def draw_codes_gate(key, part):
    key = jax.random.fold_in(key, 1)
    uniform_draw = jax.random.uniform(key, (D, FF), jnp.float32)
    return jnp.minimum(jnp.floor(uniform_draw * 4.0), 3.0).astype(jnp.bfloat16)


def draw_codes_up(key, part):
    key = jax.random.fold_in(key, 2)
    uniform_draw = jax.random.uniform(key, (D, FF), jnp.float32)
    return jnp.minimum(jnp.floor(uniform_draw * 4.0), 3.0).astype(jnp.bfloat16)


def block_levels(stream_key, extent, shards, smallest, top_value):
    def one(axis_at, blocks):
        draws = jax.random.uniform(jax.random.fold_in(jax.random.fold_in(stream_key, 6), axis_at), (blocks,), jnp.float32, smallest / len(shards), top_value / len(shards))
        return jnp.repeat(jnp.exp(draws), extent[axis_at] // blocks).reshape((-1,) + (1,) * (len(extent) - axis_at - 1))

    level = one(*shards[0])
    for cut in shards[1:]:
        level = level * one(*cut)
    return level


def normal_values(rng, extent, scale, limit, shards=(), kind=jnp.bfloat16):
    entries = scale * jax.random.normal(rng, extent, jnp.float32)
    if shards:
        entries = entries * block_levels(rng, extent, shards, -0.22, 0.18)
    return jnp.clip(entries, -limit, limit).astype(kind)


def setup_inputs(seed: int = 0, part: int = 0) -> dict:
    keys = jax.random.split(jax.random.key(seed), 9)
    part_keys = jax.random.split(jax.random.fold_in(keys[8], part), 9)
    tokens = normal_values(part_keys[0], (TOKENS, D), 1.0, 6.0, ((0, 4), (1, 4)))
    codes_gate = draw_codes_gate(jax.random.fold_in(keys[8], 71), part)
    codes_up = draw_codes_up(jax.random.fold_in(keys[8], 71), part)
    scale_gate = jnp.clip(jnp.exp(math.log(0.03) - 2.3025851 * jax.random.uniform(keys[3], (D // GROUP, FF), jnp.float32) ** block_levels(keys[3], (D // GROUP, FF), ((0, 4), (1, 4)), -0.2, 0.2)), 0.003, 0.03)
    offset_gate = jnp.clip(0.03 * jax.random.uniform(keys[4], (D // GROUP, FF), jnp.float32) ** block_levels(keys[4], (D // GROUP, FF), ((0, 4), (1, 4)), -0.2, 0.2), 0.0, 0.03)
    scale_up = jnp.clip(jnp.exp(math.log(0.03) - 2.3025851 * jax.random.uniform(keys[5], (D // GROUP, FF), jnp.float32) ** block_levels(keys[5], (D // GROUP, FF), ((0, 4), (1, 4)), -0.2, 0.2)), 0.003, 0.03)
    offset_up = jnp.clip(0.03 * jax.random.uniform(keys[6], (D // GROUP, FF), jnp.float32) ** block_levels(keys[6], (D // GROUP, FF), ((0, 4), (1, 4)), -0.2, 0.2), 0.0, 0.03)
    grad_hidden = normal_values(part_keys[7], (TOKENS, FF), 0.003, 0.046875, ((0, 4), (1, 4)))
    return dict(tokens=tokens, codes_gate=codes_gate, codes_up=codes_up, scale_gate=scale_gate, offset_gate=offset_gate, scale_up=scale_up, offset_up=offset_up, grad_hidden=grad_hidden)


def dequant(code_tile, scale_tile, offset):
    levels = code_tile.astype(jnp.float32).reshape(-1, GROUP, code_tile.shape[1])
    weight = levels * scale_tile[:, None, :] - offset[:, None, :]
    return weight.reshape(code_tile.shape).astype(jnp.bfloat16)


def group_grads(wgrad, code_tile):
    levels = code_tile.astype(jnp.float32).reshape(-1, GROUP, code_tile.shape[1])
    grouped = wgrad.reshape(levels.shape)
    return jnp.sum(grouped * levels, axis=1), -jnp.sum(grouped, axis=1)


def reference(tokens, codes_gate, codes_up, scale_gate, offset_gate, scale_up, offset_up, grad_hidden):
    block_cols = FF // 8

    def column_block(block_id):
        first_col = (block_id * block_cols).astype(jnp.int32)

        def cut(array):
            return lax.dynamic_slice_in_dim(array, first_col, block_cols, 1)

        code_g = cut(codes_gate)
        code_u = cut(codes_up)
        w_gate = dequant(code_g, cut(scale_gate), cut(offset_gate))
        w_up = dequant(code_u, cut(scale_up), cut(offset_up))
        gate_sum = jnp.dot(tokens, w_gate, preferred_element_type=jnp.float32)
        up_sum = jnp.dot(tokens, w_up, preferred_element_type=jnp.float32)
        sigmoid_gate = jax.nn.sigmoid(gate_sum)
        activation = gate_sum * sigmoid_gate
        hidden = (activation * up_sum).astype(jnp.bfloat16)
        cotangent = cut(grad_hidden).astype(jnp.float32)
        slope_term = sigmoid_gate * (1.0 + gate_sum * (1.0 - sigmoid_gate))
        grad_gate = (cotangent * up_sum * slope_term).astype(jnp.bfloat16)
        grad_up = (cotangent * activation).astype(jnp.bfloat16)
        wgrad_gate = jnp.dot(tokens.T, grad_gate, preferred_element_type=jnp.float32)
        wgrad_up = jnp.dot(tokens.T, grad_up, preferred_element_type=jnp.float32)
        scale_g, offset_g = group_grads(wgrad_gate, code_g)
        scale_u, offset_u = group_grads(wgrad_up, code_u)
        return hidden, scale_g, offset_g, scale_u, offset_u

    stacked = lax.map(column_block, jnp.arange(8, dtype=jnp.int32))

    def join(array):
        return jnp.moveaxis(array, 0, 1).reshape(array.shape[1], FF)

    return join(stacked[0]), join(stacked[1]), join(stacked[2]), join(stacked[3]), join(stacked[4])
```

```python
import functools

import jax
import jax.numpy as jnp
from jax import lax
from jax.experimental import pallas as pl
from jax.experimental.pallas import tpu as pltpu
from jax.sharding import PartitionSpec as P

GROUP = 128
MESH = pl.DeviceIdType.MESH


def body(
    dims,
    tokens_ref, fwd_gate, fwd_up, scale_gate, offset_gate, scale_up, offset_up,
    cot_ref, bwd_gate, bwd_up,
    hidden_ref, gs_gate, go_gate, gs_up, go_up,
    tok, tok_t, acc, core_out, core_in, x_out, x_in, mine, grads,
    tok_send, tok_recv, core_send, core_recv, x_send, x_recv,
    ag_send, ag_recv, mate_send, mate_recv,
):
    Z, X, J, rows, width = dims
    step = pl.program_id(0)
    z = lax.axis_index("row")
    col = lax.axis_index("col")
    x, c = col // 2, lax.rem(col, 2)
    mate = x * 2 + 1 - c
    z_rows, depth = tokens_ref.shape
    total = Z * z_rows

    def peer(o):
        return lax.rem(x + o, X)

    def to(src, dst, send, recv, axis, index):
        return pltpu.make_async_remote_copy(
            src_ref=src, dst_ref=dst, send_sem=send, recv_sem=recv,
            device_id={axis: index}, device_id_type=MESH,
        )

    def token_copy(o):
        place = pl.ds(pl.multiple_of(z * z_rows, z_rows), z_rows)
        return to(tokens_ref, tok.at[place, :], tok_send.at[o - 1], tok_recv.at[o - 1],
                  "row", lax.rem(z + o, Z))

    def core_copy(j):
        return to(core_out.at[j], core_in.at[j], core_send.at[j], core_recv.at[j], "col", mate)

    def x_copy(j, o):
        return to(x_out.at[j, o - 1], x_in.at[j, o - 1], x_send.at[j, o - 1],
                  x_recv.at[j, o - 1], "col", peer(o) * 2 + c)

    def grad_copy(j, o):
        block = grads.at[j, x * 2 + c]
        return to(block, block, ag_send.at[j, o - 1], ag_recv.at[j, o - 1],
                  "col", peer(o) * 2 + c)

    def mate_copy(j, o):
        block = grads.at[j, lax.rem(x + X - o, X) * 2 + c]
        return to(block, block, mate_send.at[j, o], mate_recv.at[j, o], "col", mate)

    @pl.when(step == 0)
    def _():
        barrier = pltpu.get_barrier_semaphore()
        for o in range(1, Z):
            pl.semaphore_signal(barrier, inc=1, device_id={"row": lax.rem(z + o, Z)},
                                device_id_type=MESH)
        for o in range(1, X):
            pl.semaphore_signal(barrier, inc=1, device_id={"col": peer(o) * 2 + c},
                                device_id_type=MESH)
        pl.semaphore_signal(barrier, inc=1, device_id={"col": mate}, device_id_type=MESH)
        pl.semaphore_wait(barrier, Z + X - 1)
        for o in range(1, Z):
            token_copy(o).start()
        tok[pl.ds(pl.multiple_of(z * z_rows, z_rows), z_rows), :] = tokens_ref[...]
        for o in range(1, Z):
            token_copy(o).wait()
        for k in range(0, depth, 512):
            tok_t[k:k + 512, :] = tok[:, k:k + 512].astype(jnp.float32).T.astype(jnp.bfloat16)

    @pl.when((step >= 1) & (step < J + 1))
    def _():
        j = step - 1
        slot = lax.rem(j, 2)
        core_copy(j).wait_recv()
        for o in range(1, X):
            xp = peer(o)
            for m in range(2):
                x_out[j, o - 1, m] = (
                    acc[slot, m, xp * 2 + c] + core_in[j, m, xp].astype(jnp.float32)
                ).astype(jnp.bfloat16)
            x_copy(j, o).start()
        for m in range(2):
            mine[slot, m] = acc[slot, m, x * 2 + c] + core_in[j, m, x].astype(jnp.float32)

    @pl.when((step >= 2) & (step < J + 2))
    def _():
        j = step - 2
        slot = lax.rem(j, 2)
        gate, up = mine[slot, 0], mine[slot, 1]
        for o in range(1, X):
            x_copy(j, o).wait_recv()
            gate = gate + x_in[j, o - 1, 0].astype(jnp.float32)
            up = up + x_in[j, o - 1, 1].astype(jnp.float32)
        sigmoid = jax.nn.sigmoid(gate)
        activation = gate * sigmoid
        hidden_ref[...] = (activation * up).astype(jnp.bfloat16)
        upstream = cot_ref[...].astype(jnp.float32)
        slope = sigmoid * (1.0 + gate * (1.0 - sigmoid))
        grads[j, col, 0] = (upstream * up * slope).astype(jnp.bfloat16)
        grads[j, col, 1] = (upstream * activation).astype(jnp.bfloat16)
        for o in range(1, X):
            grad_copy(j, o).start()
        mate_copy(j, 0).start()

    @pl.when(step < J)
    def _():
        j = step
        slot = lax.rem(j, 2)
        for m, (codes, scale, offset) in enumerate(
            ((fwd_gate, scale_gate, offset_gate), (fwd_up, scale_up, offset_up))
        ):
            part = None
            for k in range(0, depth, 512):
                pieces = []
                for g in range(k // GROUP, (k + 512) // GROUP):
                    levels = codes[g * GROUP:(g + 1) * GROUP, :].astype(jnp.float32)
                    pieces.append(
                        (levels * scale[g:g + 1, :] - offset[g:g + 1, :]).astype(jnp.bfloat16)
                    )
                term = jnp.dot(tok[:, k:k + 512], jnp.concatenate(pieces, axis=0),
                               preferred_element_type=jnp.float32)
                part = term if part is None else part + term
            acc[slot, m] = part.reshape(2 * X, rows, width)
            for xp in range(X):
                core_out[j, m, xp] = acc[slot, m, xp * 2 + 1 - c].astype(jnp.bfloat16)
        core_copy(j).start()

    @pl.when(step >= 4)
    def _():
        j = step - 4
        for o in range(X):
            mate_copy(j, o).wait()
        for o in range(1, X):
            x_copy(j, o).wait_send()
            grad_copy(j, o).wait_send()
        core_copy(j).wait_send()
        for m, (codes, gs, go) in enumerate(((bwd_gate, gs_gate, go_gate), (bwd_up, gs_up, go_up))):
            grad = grads[j, :, m].reshape(total, width)
            for k in range(0, depth, 512):
                wgrad = jnp.dot(tok_t[k:k + 512, :], grad, preferred_element_type=jnp.float32)
                levels = codes[k:k + 512, :].astype(jnp.float32)
                count = 512 // GROUP
                first = k // GROUP
                gs[first:first + count, :] = jnp.sum(
                    (wgrad * levels).reshape(count, GROUP, width), axis=1)
                go[first:first + count, :] = -jnp.sum(
                    wgrad.reshape(count, GROUP, width), axis=1)

    @pl.when((step >= 3) & (step < J + 3))
    def _():
        j = step - 3
        for o in range(1, X):
            grad_copy(j, o).wait_recv()
            mate_copy(j, o).start()


def solution(mesh):
    Z, X = mesh.shape["row"], mesh.shape["col"] // 2

    def on_device(tokens, codes_gate, codes_up, scale_gate, offset_gate, scale_up, offset_up,
                  grad_hidden):
        z_rows, depth = tokens.shape
        rows, n = grad_hidden.shape
        width = 512 if n % 512 == 0 else 256
        J = n // width
        groups = scale_gate.shape[0]
        total = Z * z_rows
        bf16, f32 = jnp.bfloat16, jnp.float32

        def at(lag):
            return lambda s: (0, jnp.clip(s - lag, 0, J - 1))

        codes_fwd = pl.BlockSpec((depth, width), at(0))
        codes_bwd = pl.BlockSpec((depth, width), at(4))
        steps_fwd = pl.BlockSpec((groups, width), at(0))
        steps_bwd = pl.BlockSpec((groups, width), at(4))
        token_rows = pl.BlockSpec((rows, width), at(2))
        dma = pltpu.SemaphoreType.DMA
        macs = 4 * total * depth * n
        return pl.pallas_call(
            functools.partial(body, (Z, X, J, rows, width)),
            grid=(J + 4,),
            out_shape=[
                jax.ShapeDtypeStruct((rows, n), bf16),
            ] + [jax.ShapeDtypeStruct((groups, n), f32)] * 4,
            in_specs=[
                pl.BlockSpec((z_rows, depth), lambda s: (0, 0)),
                codes_fwd, codes_fwd, steps_fwd, steps_fwd, steps_fwd, steps_fwd,
                token_rows, codes_bwd, codes_bwd,
            ],
            out_specs=[token_rows] + [steps_bwd] * 4,
            scratch_shapes=[
                pltpu.VMEM((total, depth), bf16),
                pltpu.VMEM((depth, total), bf16),
                pltpu.VMEM((2, 2, 2 * X, rows, width), f32),
                pltpu.VMEM((J, 2, X, rows, width), bf16),
                pltpu.VMEM((J, 2, X, rows, width), bf16),
                pltpu.VMEM((J, X - 1, 2, rows, width), bf16),
                pltpu.VMEM((J, X - 1, 2, rows, width), bf16),
                pltpu.VMEM((2, 2, rows, width), f32),
                pltpu.VMEM((J, 2 * X, 2, rows, width), bf16),
                dma((Z - 1,)), dma((Z - 1,)),
                dma((J,)), dma((J,)),
                dma((J, X - 1)), dma((J, X - 1)),
                dma((J, X - 1)), dma((J, X - 1)),
                dma((J, X)), dma((J, X)),
            ],
            compiler_params=pltpu.CompilerParams(
                collective_id=0, has_side_effects=True, vmem_limit_bytes=60 * 1024 * 1024,
            ),
            cost_estimate=pl.CostEstimate(
                flops=2 * macs, bytes_accessed=8 * depth * n, transcendentals=rows * n),
        )(tokens, codes_gate, codes_up, scale_gate, offset_gate, scale_up, offset_up,
          grad_hidden, codes_gate, codes_up)

    rows_by_group = P(("groups", "col"), "row")
    weights = P("col", "row")
    return jax.shard_map(
        on_device,
        mesh=mesh,
        in_specs=(P(("groups", "row"), "col"),) + (weights,) * 6 + (rows_by_group,),
        out_specs=(rows_by_group,) * 5,
        check_vma=False,
    )
```

```python
import functools

import jax
import jax.numpy as jnp
from jax import lax
from jax.experimental import pallas as pl
from jax.experimental.pallas import tpu as pltpu
from jax.sharding import PartitionSpec as P

GROUP = 128
MESH = pl.DeviceIdType.MESH
ACT, PASS_ON, BACK = 3, 5, 6
KEPT = 4


def body(
    dims,
    tokens_ref, fwd_gate, fwd_up, scale_gate, offset_gate, scale_up, offset_up,
    cot_ref, bwd_gate, bwd_up,
    hidden_ref, gs_gate, go_gate, gs_up, go_up,
    tok, tok_t, acc, core_out, core_in, x_out, x_in, mine, grads,
    tok_send, tok_recv, core_send, core_recv, x_send, x_recv,
    ag_send, ag_recv, mate_send, mate_recv,
):
    Z, X, J, rows, width = dims
    step = pl.program_id(0)
    z = lax.axis_index("row")
    col = lax.axis_index("col")
    x, c = col // 2, lax.rem(col, 2)
    mate = x * 2 + 1 - c
    z_rows, depth = tokens_ref.shape
    total = Z * z_rows

    def peer(o):
        return lax.rem(x + o, X)

    def to(src, dst, send, recv, axis, index):
        return pltpu.make_async_remote_copy(
            src_ref=src, dst_ref=dst, send_sem=send, recv_sem=recv,
            device_id={axis: index}, device_id_type=MESH,
        )

    piece = z_rows // 2

    def token_copy(way, h, half, block_of):
        owner = jnp.clip(block_of - way * h, 0, Z - 1)
        place = tok.at[pl.ds(pl.multiple_of(owner * z_rows + half * piece, piece), piece), :]
        lane = 0 if way == 1 else 1
        return to(place, place, tok_send.at[lane, h, half], tok_recv.at[lane, h, half],
                  "row", jnp.clip(z + way, 0, Z - 1))

    def core_copy(j):
        return to(core_out.at[j], core_in.at[j], core_send.at[j], core_recv.at[j], "col", mate)

    def x_copy(j, o):
        return to(x_out.at[j, o - 1], x_in.at[j, o - 1], x_send.at[j, o - 1],
                  x_recv.at[j, o - 1], "col", peer(o) * 2 + c)

    def grad_copy(j, o):
        block = grads.at[j, x * 2 + c]
        return to(block, block, ag_send.at[j, o - 1], ag_recv.at[j, o - 1],
                  "col", peer(o) * 2 + c)

    def mate_copy(j, o):
        block = grads.at[j, lax.rem(x + X - o, X) * 2 + c]
        return to(block, block, mate_send.at[j, o], mate_recv.at[j, o], "col", mate)

    @pl.when(step == 0)
    def _():
        barrier = pltpu.get_barrier_semaphore()
        for way in (1, -1):
            @pl.when((z + way >= 0) & (z + way < Z))
            def _(way=way):
                pl.semaphore_signal(barrier, inc=1,
                                    device_id={"row": jnp.clip(z + way, 0, Z - 1)},
                                    device_id_type=MESH)
        for o in range(1, X):
            pl.semaphore_signal(barrier, inc=1, device_id={"col": peer(o) * 2 + c},
                                device_id_type=MESH)
        pl.semaphore_signal(barrier, inc=1, device_id={"col": mate}, device_id_type=MESH)
        tok[pl.ds(pl.multiple_of(z * z_rows, z_rows), z_rows), :] = tokens_ref[...]
        ends = jnp.where(z == 0, 1, 0) + jnp.where(z == Z - 1, 1, 0)
        pl.semaphore_wait(barrier, X + 2 - ends)

        def sends(way, h):
            return (z - way * h >= 0) & (z - way * h < Z) & (z + way >= 0) & (z + way < Z)

        def takes(way, h):
            return (z - way * (h + 1) >= 0) & (z - way * (h + 1) < Z)

        for h in range(Z - 1):
            for half in range(2):
                for way in (1, -1):
                    if h:
                        @pl.when(takes(way, h - 1))
                        def _(way=way):
                            token_copy(way, h - 1, half, z - way).wait_recv()

                    @pl.when(sends(way, h))
                    def _(way=way):
                        token_copy(way, h, half, z).start()
        for half in range(2):
            for way in (1, -1):
                @pl.when(takes(way, Z - 2))
                def _(way=way):
                    token_copy(way, Z - 2, half, z - way).wait_recv()

    @pl.when(step == 2)
    def _():
        for way in (1, -1):
            for h in range(Z - 1):
                @pl.when((z - way * h >= 0) & (z - way * h < Z) & (z + way >= 0) & (z + way < Z))
                def _(way=way, h=h):
                    for half in range(2):
                        token_copy(way, h, half, z).wait_send()
        for k in range(0, depth, 512):
            tok_t[k:k + 512, :] = tok[:, k:k + 512].astype(jnp.float32).T.astype(jnp.bfloat16)

    @pl.when((step >= 1) & (step < J + 1))
    def _():
        j = step - 1
        slot = lax.rem(j, 2)
        core_copy(j).wait_recv()
        for o in range(1, X):
            xp = peer(o)
            for m in range(2):
                x_out[j, o - 1, m] = (
                    acc[slot, m, xp * 2 + c] + core_in[j, m, xp].astype(jnp.float32)
                ).astype(jnp.bfloat16)
            x_copy(j, o).start()
        for m in range(2):
            mine[lax.rem(j, KEPT), m] = acc[slot, m, x * 2 + c] + core_in[j, m, x].astype(jnp.float32)

    @pl.when((step >= ACT) & (step < J + ACT))
    def _():
        j = step - ACT
        slot = lax.rem(j, KEPT)
        gate, up = mine[slot, 0], mine[slot, 1]
        for o in range(1, X):
            x_copy(j, o).wait_recv()
            gate = gate + x_in[j, o - 1, 0].astype(jnp.float32)
            up = up + x_in[j, o - 1, 1].astype(jnp.float32)
        sigmoid = jax.nn.sigmoid(gate)
        activation = gate * sigmoid
        hidden_ref[...] = (activation * up).astype(jnp.bfloat16)
        upstream = cot_ref[...].astype(jnp.float32)
        slope = sigmoid * (1.0 + gate * (1.0 - sigmoid))
        grads[j, col, 0] = (upstream * up * slope).astype(jnp.bfloat16)
        grads[j, col, 1] = (upstream * activation).astype(jnp.bfloat16)
        for o in range(1, X):
            grad_copy(j, o).start()
        mate_copy(j, 0).start()

    @pl.when(step < J)
    def _():
        j = step
        slot = lax.rem(j, 2)
        for m, (codes, scale, offset) in enumerate(
            ((fwd_gate, scale_gate, offset_gate), (fwd_up, scale_up, offset_up))
        ):
            part = None
            for k in range(0, depth, 512):
                pieces = []
                for g in range(k // GROUP, (k + 512) // GROUP):
                    levels = codes[g * GROUP:(g + 1) * GROUP, :].astype(jnp.float32)
                    pieces.append(
                        (levels * scale[g:g + 1, :] - offset[g:g + 1, :]).astype(jnp.bfloat16)
                    )
                term = jnp.dot(tok[:, k:k + 512], jnp.concatenate(pieces, axis=0),
                               preferred_element_type=jnp.float32)
                part = term if part is None else part + term
            acc[slot, m] = part.reshape(2 * X, rows, width)
            for xp in range(X):
                core_out[j, m, xp] = acc[slot, m, xp * 2 + 1 - c].astype(jnp.bfloat16)
        core_copy(j).start()

    @pl.when(step >= BACK)
    def _():
        j = step - BACK
        for o in range(X):
            mate_copy(j, o).wait()
        for o in range(1, X):
            x_copy(j, o).wait_send()
            grad_copy(j, o).wait_send()
        core_copy(j).wait_send()
        for m, (codes, gs, go) in enumerate(((bwd_gate, gs_gate, go_gate), (bwd_up, gs_up, go_up))):
            grad = grads[j, :, m].reshape(total, width)
            for k in range(0, depth, 512):
                wgrad = jnp.dot(tok_t[k:k + 512, :], grad, preferred_element_type=jnp.float32)
                levels = codes[k:k + 512, :].astype(jnp.float32)
                count = 512 // GROUP
                first = k // GROUP
                gs[first:first + count, :] = jnp.sum(
                    (wgrad * levels).reshape(count, GROUP, width), axis=1)
                go[first:first + count, :] = -jnp.sum(
                    wgrad.reshape(count, GROUP, width), axis=1)

    @pl.when((step >= PASS_ON) & (step < J + PASS_ON))
    def _():
        j = step - PASS_ON
        for o in range(1, X):
            grad_copy(j, o).wait_recv()
            mate_copy(j, o).start()


def deliver(*refs):
    for i in range(5):
        refs[5 + i][...] = refs[i][...]


def solution(mesh):
    Z, X = mesh.shape["row"], mesh.shape["col"] // 2

    def on_device(tokens, codes_gate, codes_up, scale_gate, offset_gate, scale_up, offset_up,
                  grad_hidden):
        z_rows, depth = tokens.shape
        rows, n = grad_hidden.shape
        width = 256
        J = n // width
        groups = scale_gate.shape[0]
        total = Z * z_rows
        bf16, f32 = jnp.bfloat16, jnp.float32

        def at(lag):
            return lambda s: (0, jnp.clip(s - lag, 0, J - 1))

        codes_fwd = pl.BlockSpec((depth, width), at(0))
        codes_bwd = pl.BlockSpec((depth, width), at(BACK))
        steps_fwd = pl.BlockSpec((groups, width), at(0))
        steps_bwd = pl.BlockSpec((groups, width), at(BACK))
        token_rows = pl.BlockSpec((rows, width), at(ACT))
        dma = pltpu.SemaphoreType.DMA
        macs = 4 * total * depth * n
        results = pl.pallas_call(
            functools.partial(body, (Z, X, J, rows, width)),
            grid=(J + BACK,),
            out_shape=[
                jax.ShapeDtypeStruct((rows, n), bf16),
            ] + [jax.ShapeDtypeStruct((groups, n), f32)] * 4,
            in_specs=[
                pl.BlockSpec((z_rows, depth), lambda s: (0, 0)),
                codes_fwd, codes_fwd, steps_fwd, steps_fwd, steps_fwd, steps_fwd,
                token_rows, codes_bwd, codes_bwd,
            ],
            out_specs=[token_rows] + [steps_bwd] * 4,
            scratch_shapes=[
                pltpu.VMEM((total, depth), bf16),
                pltpu.VMEM((depth, total), bf16),
                pltpu.VMEM((2, 2, 2 * X, rows, width), f32),
                pltpu.VMEM((J, 2, X, rows, width), bf16),
                pltpu.VMEM((J, 2, X, rows, width), bf16),
                pltpu.VMEM((J, X - 1, 2, rows, width), bf16),
                pltpu.VMEM((J, X - 1, 2, rows, width), bf16),
                pltpu.VMEM((KEPT, 2, rows, width), f32),
                pltpu.VMEM((J, 2 * X, 2, rows, width), bf16),
                dma((2, Z - 1, 2)), dma((2, Z - 1, 2)),
                dma((J,)), dma((J,)),
                dma((J, X - 1)), dma((J, X - 1)),
                dma((J, X - 1)), dma((J, X - 1)),
                dma((J, X)), dma((J, X)),
            ],
            compiler_params=pltpu.CompilerParams(
                collective_id=0, has_side_effects=True, vmem_limit_bytes=60 * 1024 * 1024,
            ),
            cost_estimate=pl.CostEstimate(
                flops=2 * macs, bytes_accessed=8 * depth * n, transcendentals=rows * n),
        )(tokens, codes_gate, codes_up, scale_gate, offset_gate, scale_up, offset_up,
          grad_hidden, codes_gate, codes_up)
        part = n // 7
        blocks = [pl.BlockSpec((r.shape[0], part), lambda s: (0, s)) for r in results]
        return pl.pallas_call(
            deliver,
            grid=(7,),
            out_shape=[jax.ShapeDtypeStruct(r.shape, r.dtype) for r in results],
            in_specs=blocks,
            out_specs=blocks,
        )(*results)

    rows_by_group = P(("groups", "col"), "row")
    weights = P("col", "row")
    return jax.shard_map(
        on_device,
        mesh=mesh,
        in_specs=(P(("groups", "row"), "col"),) + (weights,) * 6 + (rows_by_group,),
        out_specs=(rows_by_group,) * 5,
        check_vma=False,
    )
```

```python
import functools

import jax
import jax.numpy as jnp
from jax import lax
from jax.experimental import pallas as pl
from jax.experimental.pallas import tpu as pltpu
from jax.sharding import PartitionSpec as P

GROUP = 128
MESH = pl.DeviceIdType.MESH
ACT, PASS_ON, BACK = 2, 4, 5
KEPT = 4


def body(
    dims,
    tokens_ref, fwd_gate, fwd_up, scale_gate, offset_gate, scale_up, offset_up,
    cot_ref, bwd_gate, bwd_up,
    hidden_ref, gs_gate, go_gate, gs_up, go_up,
    tok, tok_t, acc, core_out, core_in, x_out, x_in, mine, grads,
    tok_send, tok_recv, core_send, core_recv, x_send, x_recv,
    ag_send, ag_recv, mate_send, mate_recv,
):
    Z, X, J, rows, width = dims
    step = pl.program_id(0)
    z = lax.axis_index("row")
    col = lax.axis_index("col")
    x, c = col // 2, lax.rem(col, 2)
    mate = x * 2 + 1 - c
    z_rows, depth = tokens_ref.shape
    total = Z * z_rows

    def peer(o):
        return lax.rem(x + o, X)

    def to(src, dst, send, recv, axis, index):
        return pltpu.make_async_remote_copy(
            src_ref=src, dst_ref=dst, send_sem=send, recv_sem=recv,
            device_id={axis: index}, device_id_type=MESH,
        )

    piece = z_rows // 2

    def token_copy(way, h, half, block_of):
        owner = jnp.clip(block_of - way * h, 0, Z - 1)
        place = tok.at[pl.ds(pl.multiple_of(owner * z_rows + half * piece, piece), piece), :]
        lane = 0 if way == 1 else 1
        return to(place, place, tok_send.at[lane, h, half], tok_recv.at[lane, h, half],
                  "row", jnp.clip(z + way, 0, Z - 1))

    def core_copy(j):
        return to(core_out.at[j], core_in.at[j], core_send.at[j], core_recv.at[j], "col", mate)

    def x_copy(j, o):
        return to(x_out.at[j, o - 1], x_in.at[j, o - 1], x_send.at[j, o - 1],
                  x_recv.at[j, o - 1], "col", peer(o) * 2 + c)

    def grad_copy(j, o):
        block = grads.at[j, x * 2 + c]
        return to(block, block, ag_send.at[j, o - 1], ag_recv.at[j, o - 1],
                  "col", peer(o) * 2 + c)

    def mate_copy(j, o):
        block = grads.at[j, lax.rem(x + X - o, X) * 2 + c]
        return to(block, block, mate_send.at[j, o], mate_recv.at[j, o], "col", mate)

    @pl.when(step == 0)
    def _():
        barrier = pltpu.get_barrier_semaphore()
        for way in (1, -1):
            @pl.when((z + way >= 0) & (z + way < Z))
            def _(way=way):
                pl.semaphore_signal(barrier, inc=1,
                                    device_id={"row": jnp.clip(z + way, 0, Z - 1)},
                                    device_id_type=MESH)
        for o in range(1, X):
            pl.semaphore_signal(barrier, inc=1, device_id={"col": peer(o) * 2 + c},
                                device_id_type=MESH)
        pl.semaphore_signal(barrier, inc=1, device_id={"col": mate}, device_id_type=MESH)
        tok[pl.ds(pl.multiple_of(z * z_rows, z_rows), z_rows), :] = tokens_ref[...]
        ends = jnp.where(z == 0, 1, 0) + jnp.where(z == Z - 1, 1, 0)
        pl.semaphore_wait(barrier, X + 2 - ends)

        def sends(way, h):
            return (z - way * h >= 0) & (z - way * h < Z) & (z + way >= 0) & (z + way < Z)

        def takes(way, h):
            return (z - way * (h + 1) >= 0) & (z - way * (h + 1) < Z)

        for h in range(Z - 1):
            for half in range(2):
                for way in (1, -1):
                    if h:
                        @pl.when(takes(way, h - 1))
                        def _(way=way):
                            token_copy(way, h - 1, half, z - way).wait_recv()

                    @pl.when(sends(way, h))
                    def _(way=way):
                        token_copy(way, h, half, z).start()
        for half in range(2):
            for way in (1, -1):
                @pl.when(takes(way, Z - 2))
                def _(way=way):
                    token_copy(way, Z - 2, half, z - way).wait_recv()

    @pl.when(step == 2)
    def _():
        for way in (1, -1):
            for h in range(Z - 1):
                @pl.when((z - way * h >= 0) & (z - way * h < Z) & (z + way >= 0) & (z + way < Z))
                def _(way=way, h=h):
                    for half in range(2):
                        token_copy(way, h, half, z).wait_send()
        for k in range(0, depth, 512):
            tok_t[k:k + 512, :] = tok[:, k:k + 512].astype(jnp.float32).T.astype(jnp.bfloat16)

    @pl.when((step >= 1) & (step < J + 1))
    def _():
        j = step - 1
        slot = lax.rem(j, 2)
        core_copy(j).wait_recv()
        for o in range(1, X):
            xp = peer(o)
            for m in range(2):
                x_out[j, o - 1, m] = (
                    acc[slot, m, xp * 2 + c] + core_in[j, m, xp].astype(jnp.float32)
                ).astype(jnp.bfloat16)
            x_copy(j, o).start()
        for m in range(2):
            mine[lax.rem(j, KEPT), m] = acc[slot, m, x * 2 + c] + core_in[j, m, x].astype(jnp.float32)

    @pl.when((step >= ACT) & (step < J + ACT))
    def _():
        j = step - ACT
        slot = lax.rem(j, KEPT)
        gate, up = mine[slot, 0], mine[slot, 1]
        for o in range(1, X):
            x_copy(j, o).wait_recv()
            gate = gate + x_in[j, o - 1, 0].astype(jnp.float32)
            up = up + x_in[j, o - 1, 1].astype(jnp.float32)
        sigmoid = jax.nn.sigmoid(gate)
        activation = gate * sigmoid
        hidden_ref[...] = (activation * up).astype(jnp.bfloat16)
        upstream = cot_ref[...].astype(jnp.float32)
        slope = sigmoid * (1.0 + gate * (1.0 - sigmoid))
        grads[j, col, 0] = (upstream * up * slope).astype(jnp.bfloat16)
        grads[j, col, 1] = (upstream * activation).astype(jnp.bfloat16)
        for o in range(1, X):
            grad_copy(j, o).start()
        mate_copy(j, 0).start()

    @pl.when(step < J)
    def _():
        j = step
        slot = lax.rem(j, 2)
        for m, (codes, scale, offset) in enumerate(
            ((fwd_gate, scale_gate, offset_gate), (fwd_up, scale_up, offset_up))
        ):
            part = None
            for k in range(0, depth, 512):
                pieces = []
                for g in range(k // GROUP, (k + 512) // GROUP):
                    levels = codes[g * GROUP:(g + 1) * GROUP, :].astype(jnp.float32)
                    pieces.append(
                        (levels * scale[g:g + 1, :] - offset[g:g + 1, :]).astype(jnp.bfloat16)
                    )
                term = jnp.dot(tok[:, k:k + 512], jnp.concatenate(pieces, axis=0),
                               preferred_element_type=jnp.float32)
                part = term if part is None else part + term
            acc[slot, m] = part.reshape(2 * X, rows, width)
            for xp in range(X):
                core_out[j, m, xp] = acc[slot, m, xp * 2 + 1 - c].astype(jnp.bfloat16)
        core_copy(j).start()

    @pl.when(step >= BACK)
    def _():
        j = step - BACK
        for o in range(X):
            mate_copy(j, o).wait()
        for o in range(1, X):
            x_copy(j, o).wait_send()
            grad_copy(j, o).wait_send()
        core_copy(j).wait_send()
        for m, (codes, gs, go) in enumerate(((bwd_gate, gs_gate, go_gate), (bwd_up, gs_up, go_up))):
            grad = grads[j, :, m].reshape(total, width)
            for k in range(0, depth, 512):
                wgrad = jnp.dot(tok_t[k:k + 512, :], grad, preferred_element_type=jnp.float32)
                levels = codes[k:k + 512, :].astype(jnp.float32)
                count = 512 // GROUP
                first = k // GROUP
                gs[first:first + count, :] = jnp.sum(
                    (wgrad * levels).reshape(count, GROUP, width), axis=1)
                go[first:first + count, :] = -jnp.sum(
                    wgrad.reshape(count, GROUP, width), axis=1)

    @pl.when((step >= PASS_ON) & (step < J + PASS_ON))
    def _():
        j = step - PASS_ON
        for o in range(1, X):
            grad_copy(j, o).wait_recv()
            mate_copy(j, o).start()


def deliver(*refs):
    for i in range(5):
        refs[5 + i][...] = refs[i][...]


def solution(mesh):
    Z, X = mesh.shape["row"], mesh.shape["col"] // 2

    def on_device(tokens, codes_gate, codes_up, scale_gate, offset_gate, scale_up, offset_up,
                  grad_hidden):
        z_rows, depth = tokens.shape
        rows, n = grad_hidden.shape
        width = 256
        J = n // width
        groups = scale_gate.shape[0]
        total = Z * z_rows
        bf16, f32 = jnp.bfloat16, jnp.float32

        def at(lag):
            return lambda s: (0, jnp.clip(s - lag, 0, J - 1))

        codes_fwd = pl.BlockSpec((depth, width), at(0))
        codes_bwd = pl.BlockSpec((depth, width), at(BACK))
        steps_fwd = pl.BlockSpec((groups, width), at(0))
        steps_bwd = pl.BlockSpec((groups, width), at(BACK))
        token_rows = pl.BlockSpec((rows, width), at(ACT))
        dma = pltpu.SemaphoreType.DMA
        macs = 4 * total * depth * n
        results = pl.pallas_call(
            functools.partial(body, (Z, X, J, rows, width)),
            grid=(J + BACK,),
            out_shape=[
                jax.ShapeDtypeStruct((rows, n), bf16),
            ] + [jax.ShapeDtypeStruct((groups, n), f32)] * 4,
            in_specs=[
                pl.BlockSpec((z_rows, depth), lambda s: (0, 0)),
                codes_fwd, codes_fwd, steps_fwd, steps_fwd, steps_fwd, steps_fwd,
                token_rows, codes_bwd, codes_bwd,
            ],
            out_specs=[token_rows] + [steps_bwd] * 4,
            scratch_shapes=[
                pltpu.VMEM((total, depth), bf16),
                pltpu.VMEM((depth, total), bf16),
                pltpu.VMEM((2, 2, 2 * X, rows, width), f32),
                pltpu.VMEM((J, 2, X, rows, width), bf16),
                pltpu.VMEM((J, 2, X, rows, width), bf16),
                pltpu.VMEM((J, X - 1, 2, rows, width), bf16),
                pltpu.VMEM((J, X - 1, 2, rows, width), bf16),
                pltpu.VMEM((KEPT, 2, rows, width), f32),
                pltpu.VMEM((J, 2 * X, 2, rows, width), bf16),
                dma((2, Z - 1, 2)), dma((2, Z - 1, 2)),
                dma((J,)), dma((J,)),
                dma((J, X - 1)), dma((J, X - 1)),
                dma((J, X - 1)), dma((J, X - 1)),
                dma((J, X)), dma((J, X)),
            ],
            compiler_params=pltpu.CompilerParams(
                collective_id=0, has_side_effects=True, vmem_limit_bytes=60 * 1024 * 1024,
            ),
            cost_estimate=pl.CostEstimate(
                flops=2 * macs, bytes_accessed=8 * depth * n, transcendentals=rows * n),
        )(tokens, codes_gate, codes_up, scale_gate, offset_gate, scale_up, offset_up,
          grad_hidden, codes_gate, codes_up)
        part = n // 2
        blocks = [pl.BlockSpec((r.shape[0], part), lambda s: (0, s)) for r in results]
        return pl.pallas_call(
            deliver,
            grid=(2,),
            out_shape=[jax.ShapeDtypeStruct(r.shape, r.dtype) for r in results],
            in_specs=blocks,
            out_specs=blocks,
        )(*results)

    rows_by_group = P(("groups", "col"), "row")
    weights = P("col", "row")
    return jax.shard_map(
        on_device,
        mesh=mesh,
        in_specs=(P(("groups", "row"), "col"),) + (weights,) * 6 + (rows_by_group,),
        out_specs=(rows_by_group,) * 5,
        check_vma=False,
    )
```
